512 devices in a mesh: dp: 32 (over y, z_lo, core), mp: 16 (over x, z_hi).
Axes of the slice: x: 4, y: 8, z: 8 (z_hi: 4, z_lo: 2; z = z_hi * 2 + z_lo), core: 2. Of those that a mesh axis runs over, the one named last changes fastest.
Arguments:
- tokens: bfloat16 [4096, 8192], P(('dp', 'mp')), may hold values from -6 to 6
- kv_weight: bfloat16 [8192, 2048], P(None, 'mp'), may hold values from -0.125 to 0.125
- out_grad: bfloat16 [4096, 2048], P('dp', 'mp'), may hold values from -6 to 6
- basis: bfloat16 [8192, 1024], P(None, 'mp'), may hold values from -0.0625 to 0.0625
- first_moment: float32 [1024, 2048], P('mp', 'dp'), may hold values from -96 to 96
- second_moment: float32 [1024, 2048], P('mp', 'dp'), may hold values from 8 to 200
Outputs:
- input_grad: bfloat16 [4096, 8192], P(('dp', 'mp'))
- update: bfloat16 [8192, 2048], P('mp', 'dp')
- new_first: float32 [1024, 2048], P('mp', 'dp')
- new_second: float32 [1024, 2048], P('mp', 'dp')
The draws below stay inside these ranges and needn't reach their ends.
All inputs are finite; a program needn't handle non-finite values.
Results may differ from the reference program's by a relative error of at most 0.023.
Values may be sent and summed in bfloat16 or wider, within the bound.
No kernel may reach another device: no remote copies, remote signals or barrier semaphores. Data moves between devices by JAX's collectives and lax.ppermute only.
A program may use at most 64 MiB of HBM per device.

```python
import math
import jax
import jax.numpy as jnp
from jax import lax

D = 8192
KV = 2048
R = 1024
STEP = 10
TOKENS = 4096
N_MP = 16


def shard_levels(stream_key, extent, split, low, top_value):
    factor_of, own = 1.0, jax.random.fold_in(stream_key, 6)
    for dim, blocks in split:
        heights = jnp.exp(jax.random.uniform(jax.random.fold_in(own, dim), (blocks,), jnp.float32, low / len(split), top_value / len(split)))
        factor_of = factor_of * jnp.repeat(heights, extent[dim] // blocks).reshape([-1 if axis == dim else 1 for axis in range(len(extent))])
    return factor_of


def scatter_about(stream_key, shape, width, reach, cuts=(), held_as=jnp.bfloat16):
    drawn = jax.random.normal(stream_key, shape, jnp.float32) * width
    if len(cuts) > 0:
        drawn = shard_levels(stream_key, shape, cuts, -0.22, 0.18) * drawn
    return jnp.clip(drawn, min=-reach, max=reach).astype(held_as)


def setup_inputs(seed: int = 0) -> dict:
    splits = jax.random.split(jax.random.key(seed), 7)
    return {
        "tokens": scatter_about(splits[0], (TOKENS, D), 1.0, 6.0, ((0, 512),)),
        "kv_weight": scatter_about(splits[1], (D, KV), KV ** -0.5, 0.125, ((1, 16),)),
        "out_grad": scatter_about(splits[2], (TOKENS, KV), 1.0, 6.0, ((0, 32), (1, 16))),
        "basis": scatter_about(splits[3], (D, R), D ** -0.5, 0.0625, ((1, 16),)),
        "first_moment": scatter_about(splits[4], (R, KV), 16.0, 96.0, ((0, 16), (1, 32)), jnp.float32),
        "second_moment": jnp.clip(jnp.exp(math.log(200.0) - 3.218876 * jax.random.uniform(splits[5], (R, KV), jnp.float32) ** shard_levels(splits[5], (R, KV), ((0, 16), (1, 32)), -0.2, 0.2)), 8.0, 200.0),
    }


epsilon = 1e-08

def reference(tokens, kv_weight, out_grad, basis, first_moment, second_moment):
    projected = jnp.dot(tokens, basis, preferred_element_type=jnp.float32).astype(jnp.bfloat16)
    subspace_grad = jnp.dot(projected.T, out_grad, preferred_element_type=jnp.float32)
    new_first = 0.9 * first_moment + 0.1 * subspace_grad
    new_second = 0.999 * second_moment + 0.001 * subspace_grad * subspace_grad
    first_scale = 1.0 - 0.9 ** STEP
    second_scale = 1.0 - 0.999 ** STEP
    direction = (new_first / first_scale / (jnp.sqrt(new_second / second_scale) + epsilon)).astype(jnp.bfloat16)
    update = jnp.dot(basis, direction, preferred_element_type=jnp.float32).astype(jnp.bfloat16)
    group_width = KV // N_MP
    summed_terms = jnp.zeros((tokens.shape[0], tokens.shape[1]), jnp.float32)
    for group in range(N_MP):
        grad_cols = out_grad[:, group * group_width:(group + 1) * group_width]
        weight_cols = kv_weight[:, group * group_width:(group + 1) * group_width]
        partial_term = lax.dot_general(grad_cols, weight_cols, (((1,), (1,)), ((), ())), preferred_element_type=jnp.float32)
        rounded = lax.optimization_barrier(partial_term.astype(jnp.bfloat16))
        summed_terms = summed_terms + rounded.astype(jnp.float32)
    input_grad = summed_terms.astype(jnp.bfloat16)
    return (input_grad, update, new_first, new_second)
```

```python
import jax
import jax.numpy as jnp
from jax import lax
from jax.sharding import PartitionSpec as P

STEP = 10


epsilon = 1e-08

X, ZH = 4, 4
GROUPS_X = [[z + ZH * x for x in range(X)] for z in range(ZH)]
GROUPS_Z = [[z + ZH * x for z in range(ZH)] for x in range(X)]


def body(tokens, kv_weight, out_grad, basis, first_moment, second_moment):
    n_mp = 16
    rows, width = tokens.shape
    block = width // n_mp
    half = block // 2
    rank = basis.shape[1]
    n_tok = out_grad.shape[0]
    cols = out_grad.shape[1]
    core = lax.axis_index("dp") % 2
    swap = [(d, d ^ 1) for d in range(32)]
    across = [[2 * k + c for k in range(16)] for c in range(2)]

    terms = lax.dot_general(
        out_grad, kv_weight, (((1,), (1,)), ((), ())), preferred_element_type=jnp.float32
    ).astype(jnp.bfloat16)
    tokens, basis, terms = lax.optimization_barrier((tokens, basis, terms))
    input_grad = lax.psum_scatter(
        terms, "mp", scatter_dimension=0, axis_index_groups=GROUPS_X, tiled=True
    )
    input_grad = lax.psum_scatter(
        input_grad, "mp", scatter_dimension=0, axis_index_groups=GROUPS_Z, tiled=True
    )

    basis_t = basis.T.reshape(rank, n_mp, 2, half)
    mine = lax.dynamic_index_in_dim(basis_t, core, 2, keepdims=False).transpose(1, 0, 2)
    tok = tokens.reshape(rows, n_mp, 2, half)
    tok_mine = lax.dynamic_index_in_dim(tok, core, 2, keepdims=False).transpose(1, 0, 2)
    tok_other = lax.dynamic_index_in_dim(tok, 1 - core, 2, keepdims=False).transpose(1, 0, 2)
    got = lax.all_to_all(
        jnp.concatenate([mine, tok_mine, tok_other], axis=1), "mp", 0, 0, tiled=True
    )
    basis_mine = got[:, :rank].reshape(n_mp * rank, half)
    tok_mine = got[:, rank : rank + rows].reshape(n_tok, half)
    tok_other = got[:, rank + rows :].reshape(n_tok, half)
    basis_other = lax.ppermute(basis_mine, "dp", swap)
    nt = (((1,), (1,)), ((), ()))
    projected = lax.dot_general(
        basis_mine, tok_mine, nt, preferred_element_type=jnp.float32
    ) + lax.dot_general(basis_other, tok_other, nt, preferred_element_type=jnp.float32)
    projected = projected.astype(jnp.bfloat16).reshape(n_mp, rank, n_tok)

    got = lax.all_to_all(
        jnp.concatenate(
            [projected, jnp.broadcast_to(out_grad[None], (n_mp, n_tok, cols))], axis=1
        ),
        "mp",
        0,
        0,
        tiled=True,
    )
    projected = got[:, :rank].astype(jnp.float32).sum(0).astype(jnp.bfloat16)
    grad_all = got[:, rank:]
    partial_grad = jnp.einsum(
        "rt,jtc->jrc", projected, grad_all, preferred_element_type=jnp.float32
    )

    theirs = lax.ppermute(partial_grad.astype(jnp.bfloat16), "dp", swap)
    both = (partial_grad + theirs.astype(jnp.float32)).astype(jnp.bfloat16)
    got = lax.all_to_all(both, "dp", 0, 0, axis_index_groups=across, tiled=True)
    summed = got.astype(jnp.float32).sum(0)
    width_c = first_moment.shape[1]
    local_grad = lax.dynamic_slice_in_dim(summed, core * width_c, width_c, 1)

    new_first = 0.9 * first_moment + 0.1 * local_grad
    new_second = 0.999 * second_moment + 0.001 * local_grad * local_grad
    first_scale = 1.0 - 0.9**STEP
    second_scale = 1.0 - 0.999**STEP
    direction = (new_first / first_scale / (jnp.sqrt(new_second / second_scale) + epsilon)).astype(
        jnp.bfloat16
    )
    everyone = lax.all_to_all(
        jnp.broadcast_to(direction[None], (n_mp,) + direction.shape), "mp", 0, 0, tiled=True
    ).reshape(n_mp * rank, width_c)
    tn = (((0,), (0,)), ((), ()))
    up_mine = lax.dot_general(basis_mine, everyone, tn, preferred_element_type=jnp.float32)
    up_other = lax.dot_general(basis_other, everyone, tn, preferred_element_type=jnp.float32)
    first_half = jnp.where(core == 0, up_mine, up_other)
    second_half = jnp.where(core == 0, up_other, up_mine)
    update = jnp.concatenate([first_half, second_half], axis=0).astype(jnp.bfloat16)
    return (input_grad, update, new_first, new_second)


def solution(mesh):
    placed = (
        P(("dp", "mp"), None),
        P(None, "mp"),
        P("dp", "mp"),
        P(None, "mp"),
        P("mp", "dp"),
        P("mp", "dp"),
    )
    return jax.shard_map(
        body,
        mesh=mesh,
        in_specs=placed,
        out_specs=(P(("dp", "mp"), None), P("mp", "dp"), P("mp", "dp"), P("mp", "dp")),
        check_vma=False,
    )
```

```python
import functools

import jax
import jax.numpy as jnp
from jax import lax
from jax.experimental import pallas as pl
from jax.experimental.pallas import tpu as pltpu
from jax.sharding import PartitionSpec as P

STEP = 10


epsilon = 1e-08

X, ZH, N_MP, N_DP, RANK = 4, 4, 16, 32, 64
ACROSS = [[2 * k + c for k in range(N_DP // 2)] for c in range(2)]
SWAP = [(d, d ^ 1) for d in range(N_DP)]
NT = (((1,), (1,)), ((), ()))
TN = (((0,), (0,)), ((), ()))
LIMIT = 48 * 2**20


def local(kernel, outs, *args, flops, moved, name):
    specs = [pl.BlockSpec(memory_space=pltpu.SMEM)] + [pl.BlockSpec(memory_space=pltpu.VMEM)] * (len(args) - 1)
    return pl.pallas_call(
        kernel,
        out_shape=outs,
        in_specs=specs,
        out_specs=jax.tree.map(lambda _: pl.BlockSpec(memory_space=pltpu.VMEM), outs),
        compiler_params=pltpu.CompilerParams(vmem_limit_bytes=LIMIT),
        cost_estimate=pl.CostEstimate(flops=flops, bytes_accessed=moved, transcendentals=0),
        name=name,
    )(*args)


def pack_rows(at_ref, basis_ref, tok_ref, out_ref):
    core = at_ref[0]
    rank, half = basis_ref.shape[0], out_ref.shape[2]
    for j in range(N_MP):
        mine = pl.ds(pl.multiple_of((2 * j + core) * half, half), half)
        other = pl.ds(pl.multiple_of((2 * j + 1 - core) * half, half), half)
        out_ref[j, :rank, :] = basis_ref[:, mine]
        out_ref[j, rank:, :] = jnp.concatenate([tok_ref[:, mine], tok_ref[:, other]], axis=0)


def adam(at_ref, got_ref, first_ref, second_ref, terms_ref, new_first_ref, new_second_ref, out_ref):
    core = at_ref[0]
    rank, width = first_ref.shape
    total = got_ref[0].astype(jnp.float32)
    for j in range(1, got_ref.shape[0]):
        total += got_ref[j].astype(jnp.float32)
    grad = jnp.where(core == 0, total[:, :width], total[:, width:])
    new_first = 0.9 * first_ref[...] + 0.1 * grad
    new_second = 0.999 * second_ref[...] + 0.001 * grad * grad
    new_first_ref[...] = new_first
    new_second_ref[...] = new_second
    first_scale = 1.0 - 0.9**STEP
    second_scale = 1.0 - 0.999**STEP
    direction = new_first / first_scale / (jnp.sqrt(new_second / second_scale) + epsilon)
    wide = jnp.concatenate([direction[: rank // 2], direction[rank // 2 :]], axis=1)
    rows = out_ref.shape[1]
    flat = jnp.concatenate(
        [wide[rows * b : rows * (b + 1)] for b in range(rank // 2 // rows)], axis=1
    ).astype(jnp.bfloat16)
    block = terms_ref.shape[2]
    for j in range(N_MP):
        out_ref[j, :, :block] = terms_ref[j]
        out_ref[j, :, block:] = flat


def finish(at_ref, mine_ref, other_ref, got_ref, input_grad_ref, update_ref):
    core = at_ref[0]
    cols, half = update_ref.shape[0], mine_ref.shape[2]
    rows, block = got_ref.shape[1], input_grad_ref.shape[1] // X
    lanes = 2 * cols
    for x in range(X):
        acc = got_ref[ZH * x, :, :block].astype(jnp.float32)
        for z in range(1, ZH):
            acc += got_ref[ZH * x + z, :, :block].astype(jnp.float32)
        input_grad_ref[:, block * x : block * (x + 1)] = acc.astype(input_grad_ref.dtype)
    parts = []
    for j in range(N_MP):
        flat = got_ref[j, :, block:].astype(jnp.float32)
        parts += [flat[:, lanes * b : lanes * (b + 1)] for b in range(RANK // 2 // rows)]
    direction = jnp.concatenate(parts, axis=0).astype(jnp.bfloat16)
    for where, ref in ((core, mine_ref), (1 - core, other_ref)):
        low = ref[:, : RANK // 2, :].reshape(N_MP * RANK // 2, half)
        high = ref[:, RANK // 2 : RANK, :].reshape(N_MP * RANK // 2, half)
        low = lax.dot_general(direction, low, TN, preferred_element_type=jnp.float32)
        high = lax.dot_general(direction, high, TN, preferred_element_type=jnp.float32)
        update_ref[:, pl.ds(pl.multiple_of(where * half, half), half)] = (
            low[:cols] + high[cols:]
        ).astype(update_ref.dtype)


def subspace(at_ref, got_ref, out_ref):
    total = got_ref[0, :RANK, :].astype(jnp.float32)
    for j in range(1, N_MP):
        total += got_ref[j, :RANK, :].astype(jnp.float32)
    projected = total.astype(jnp.bfloat16)
    for j in range(N_MP):
        out_ref[j] = jnp.dot(
            projected, got_ref[j, RANK:, :], preferred_element_type=jnp.float32
        ).astype(out_ref.dtype)


def grad_terms(at_ref, columns_ref, own_ref, *refs):
    core, x, z = at_ref[0], at_ref[1], at_ref[2]
    pieces, out_ref = refs[:-1], refs[-1]
    half = pieces[0].shape[0]
    grads = [columns_ref[((x + X - k) & (X - 1)) * ZH + z, RANK:, :] for k in range(X)]
    for where, refs in ((core, pieces[: X - 1]), (1 - core, pieces[X - 1 :])):
        rows = pl.ds(pl.multiple_of(where * half, half), half)
        acc = lax.dot_general(grads[0], own_ref[rows, :], NT, preferred_element_type=jnp.float32)
        for g, w in zip(grads[1:], refs):
            acc += lax.dot_general(g, w[...], NT, preferred_element_type=jnp.float32)
        out_ref[:, rows] = acc.astype(out_ref.dtype)


def body(tokens, kv_weight, out_grad, basis, first_moment, second_moment):
    bf16 = functools.partial(jax.ShapeDtypeStruct, dtype=jnp.bfloat16)
    f32 = functools.partial(jax.ShapeDtypeStruct, dtype=jnp.float32)
    rows, width = tokens.shape
    half = width // N_MP // 2
    n_tok, cols = out_grad.shape
    core = lax.axis_index("dp") & 1
    x, z = lax.axis_index("mp") // ZH, lax.axis_index("mp") % ZH
    at = jnp.stack([core, x, z])

    packed = local(
        pack_rows,
        bf16((N_MP, RANK + 2 * rows, half)),
        at,
        basis.T,
        tokens,
        flops=0,
        moved=2 * 2**20,
        name="pack_rows",
    )
    packed, kv_weight, out_grad = lax.optimization_barrier((packed, kv_weight, out_grad))
    mine = lax.all_to_all(packed, "mp", 0, 0, tiled=True)

    def along_x(a, k):
        return lax.ppermute(a, "mp", [(m, (m + ZH * k) % N_MP) for m in range(N_MP)])

    w_rows = width // X
    own = lax.dynamic_slice_in_dim(kv_weight, x * w_rows, w_rows, 0)

    def piece(k):
        start = (((x + k) & (X - 1)) * 2 + core) * (w_rows // 2)
        return along_x(lax.dynamic_slice_in_dim(kv_weight, start, w_rows // 2, 0), k)

    weight = [piece(k) for k in range(1, X)]
    mine, weight[0], weight[2] = lax.optimization_barrier((mine, weight[0], weight[2]))

    other = lax.ppermute(mine, "dp", SWAP)

    def block(a, lo, hi):
        return a[:, lo:hi].reshape(N_MP * (hi - lo), half)

    projected = lax.dot_general(
        block(mine, 0, RANK), block(mine, RANK, RANK + rows), NT, preferred_element_type=jnp.float32
    ) + lax.dot_general(
        block(other, 0, RANK),
        block(mine, RANK + rows, RANK + 2 * rows),
        NT,
        preferred_element_type=jnp.float32,
    )
    projected = projected.astype(jnp.bfloat16).reshape(N_MP, RANK, n_tok)

    columns = lax.all_to_all(
        jnp.concatenate(
            [projected, jnp.broadcast_to(out_grad[None], (N_MP, n_tok, cols))], axis=1
        ),
        "mp",
        0,
        0,
        tiled=True,
    )
    weight += [lax.ppermute(w, "dp", SWAP) for w in weight]
    columns, weight[1], weight[3], weight[5] = lax.optimization_barrier(
        (columns, weight[1], weight[3], weight[5])
    )
    partial_grad = local(
        subspace,
        bf16((N_MP, RANK, cols)),
        at,
        columns,
        flops=2**25,
        moved=2**20,
        name="subspace",
    )

    theirs = lax.ppermute(partial_grad, "dp", SWAP)
    both = (partial_grad.astype(jnp.float32) + theirs.astype(jnp.float32)).astype(jnp.bfloat16)
    both, columns = lax.optimization_barrier((both, columns))
    got = lax.all_to_all(both, "dp", 0, 0, axis_index_groups=ACROSS, tiled=True)

    terms = local(
        grad_terms,
        bf16((n_tok, width // X)),
        at,
        columns,
        own,
        *weight,
        flops=2 * n_tok * X * cols * width // X,
        moved=3 * 2**20,
        name="grad_terms",
    )
    packed_width = width // X + RANK // rows * first_moment.shape[1]
    new_first, new_second, packed = local(
        adam,
        (f32(first_moment.shape), f32(first_moment.shape), bf16((N_MP, rows, packed_width))),
        at,
        got,
        first_moment,
        second_moment,
        terms.reshape(N_MP, rows, width // X),
        flops=2**19,
        moved=2**20,
        name="adam",
    )
    input_grad, update = local(
        finish,
        (bf16((rows, width)), bf16((first_moment.shape[1], width // N_MP))),
        at,
        mine,
        other,
        lax.all_to_all(packed, "mp", 0, 0, tiled=True),
        flops=2 * 2**26,
        moved=2**21,
        name="finish",
    )
    return (input_grad, update.T, new_first, new_second)


def solution(mesh):
    placed = (
        P(("dp", "mp"), None),
        P(None, "mp"),
        P("dp", "mp"),
        P(None, "mp"),
        P("mp", "dp"),
        P("mp", "dp"),
    )
    return jax.shard_map(
        body,
        mesh=mesh,
        in_specs=placed,
        out_specs=(P(("dp", "mp"), None), P("mp", "dp"), P("mp", "dp"), P("mp", "dp")),
        check_vma=False,
    )
```

```python
import functools

import jax
import jax.numpy as jnp
from jax import lax
from jax.experimental import pallas as pl
from jax.experimental.pallas import tpu as pltpu
from jax.sharding import PartitionSpec as P

STEP = 10


epsilon = 1e-08

X, ZH, N_MP, N_DP, RANK = 4, 4, 16, 32, 64
GROUPS_X = [[z + ZH * x for x in range(X)] for z in range(ZH)]
GROUPS_Z = [[z + ZH * x for z in range(ZH)] for x in range(X)]
ACROSS = [[2 * k + c for k in range(N_DP // 2)] for c in range(2)]
SWAP = [(d, d ^ 1) for d in range(N_DP)]
NT = (((1,), (1,)), ((), ()))
TN = (((0,), (0,)), ((), ()))
LIMIT = 48 * 2**20


VMEM = pl.BlockSpec(memory_space=pltpu.VMEM)
HBM = pl.BlockSpec(memory_space=pltpu.HBM)


def local(kernel, outs, *args, ins, scratch=(), limit=LIMIT, flops=0, moved=0, name):
    return pl.pallas_call(
        kernel,
        out_shape=outs,
        in_specs=[pl.BlockSpec(memory_space=pltpu.SMEM), *ins],
        out_specs=jax.tree.map(lambda _: VMEM, outs),
        scratch_shapes=scratch,
        compiler_params=pltpu.CompilerParams(vmem_limit_bytes=limit),
        cost_estimate=pl.CostEstimate(flops=flops, bytes_accessed=moved, transcendentals=0),
        name=name,
    )(*args)


def pack_rows(at_ref, basis_ref, tok_ref, out_ref, tok, sems):
    core = at_ref[0]
    half = out_ref.shape[2]
    first = pltpu.make_async_copy(tok_ref, tok, sems.at[0])
    first.start()
    copies = []
    for j in range(N_MP):
        mine = pl.ds(pl.multiple_of((2 * j + core) * half, half), half)
        copies.append(
            pltpu.make_async_copy(basis_ref.at[:, mine], out_ref.at[j, pl.ds(0, RANK), :], sems.at[1])
        )
    for copy in copies:
        copy.start()
    first.wait()
    for j in range(N_MP):
        mine = pl.ds(pl.multiple_of((2 * j + core) * half, half), half)
        other = pl.ds(pl.multiple_of((2 * j + 1 - core) * half, half), half)
        out_ref[j, RANK:, :] = jnp.concatenate([tok[:, mine], tok[:, other]], axis=0)
    for copy in copies:
        copy.wait()


def adam(at_ref, got_ref, first_ref, second_ref, new_first_ref, new_second_ref, out_ref):
    core = at_ref[0]
    rank, width = first_ref.shape
    total = got_ref[0].astype(jnp.float32)
    for j in range(1, got_ref.shape[0]):
        total += got_ref[j].astype(jnp.float32)
    grad = jnp.where(core == 0, total[:, :width], total[:, width:])
    new_first = 0.9 * first_ref[...] + 0.1 * grad
    new_second = 0.999 * second_ref[...] + 0.001 * grad * grad
    new_first_ref[...] = new_first
    new_second_ref[...] = new_second
    first_scale = 1.0 - 0.9**STEP
    second_scale = 1.0 - 0.999**STEP
    direction = new_first / first_scale / (jnp.sqrt(new_second / second_scale) + epsilon)
    wide = jnp.concatenate([direction[: rank // 2], direction[rank // 2 :]], axis=1)
    rows = out_ref.shape[1]
    flat = jnp.concatenate(
        [wide[rows * b : rows * (b + 1)] for b in range(rank // 2 // rows)], axis=1
    ).astype(jnp.bfloat16)
    for j in range(N_MP):
        out_ref[j] = flat


def back_project(at_ref, mine_ref, other_ref, got_ref, update_ref):
    core = at_ref[0]
    cols, half = update_ref.shape[0], mine_ref.shape[2]
    rows = got_ref.shape[1]
    lanes = 2 * cols
    parts = []
    for j in range(N_MP):
        flat = got_ref[j].astype(jnp.float32)
        parts += [flat[:, lanes * b : lanes * (b + 1)] for b in range(RANK // 2 // rows)]
    direction = jnp.concatenate(parts, axis=0).astype(jnp.bfloat16)
    for where, ref in ((core, mine_ref), (1 - core, other_ref)):
        low = ref[:, : RANK // 2, :].reshape(N_MP * RANK // 2, half)
        high = ref[:, RANK // 2 : RANK, :].reshape(N_MP * RANK // 2, half)
        low = lax.dot_general(direction, low, TN, preferred_element_type=jnp.float32)
        high = lax.dot_general(direction, high, TN, preferred_element_type=jnp.float32)
        update_ref[:, pl.ds(pl.multiple_of(where * half, half), half)] = (
            low[:cols] + high[cols:]
        ).astype(update_ref.dtype)


def subspace(at_ref, got_ref, out_ref):
    total = got_ref[0, :RANK, :].astype(jnp.float32)
    for j in range(1, N_MP):
        total += got_ref[j, :RANK, :].astype(jnp.float32)
    projected = total.astype(jnp.bfloat16)
    for j in range(N_MP):
        out_ref[j] = jnp.dot(
            projected, got_ref[j, RANK:, :], preferred_element_type=jnp.float32
        ).astype(out_ref.dtype)


def body(tokens, kv_weight, out_grad, basis, first_moment, second_moment):
    bf16 = functools.partial(jax.ShapeDtypeStruct, dtype=jnp.bfloat16)
    f32 = functools.partial(jax.ShapeDtypeStruct, dtype=jnp.float32)
    rows, width = tokens.shape
    half = width // N_MP // 2
    n_tok, cols = out_grad.shape
    at = (lax.axis_index("dp") & 1)[None]

    packed = local(
        pack_rows,
        bf16((N_MP, RANK + 2 * rows, half)),
        at,
        basis.T,
        tokens,
        ins=[HBM] * 2,
        scratch=[pltpu.VMEM((rows, width), jnp.bfloat16), pltpu.SemaphoreType.DMA((2,))],
        limit=60 * 2**20,
        flops=0,
        moved=2 * 2**20,
        name="pack_rows",
    )
    packed, kv_weight, out_grad = lax.optimization_barrier((packed, kv_weight, out_grad))
    mine = lax.all_to_all(packed, "mp", 0, 0, tiled=True)

    terms = lax.dot_general(
        out_grad, kv_weight, (((1,), (1,)), ((), ())), preferred_element_type=jnp.float32
    ).astype(jnp.bfloat16)
    input_grad = lax.psum_scatter(
        terms, "mp", scatter_dimension=0, axis_index_groups=GROUPS_X, tiled=True
    )

    other = lax.ppermute(mine, "dp", SWAP)

    def block(a, lo, hi):
        return a[:, lo:hi].reshape(N_MP * (hi - lo), half)

    projected = lax.dot_general(
        block(mine, 0, RANK), block(mine, RANK, RANK + rows), NT, preferred_element_type=jnp.float32
    ) + lax.dot_general(
        block(other, 0, RANK),
        block(mine, RANK + rows, RANK + 2 * rows),
        NT,
        preferred_element_type=jnp.float32,
    )
    projected = projected.astype(jnp.bfloat16).reshape(N_MP, RANK, n_tok)

    columns = lax.all_to_all(
        jnp.concatenate(
            [projected, jnp.broadcast_to(out_grad[None], (N_MP, n_tok, cols))], axis=1
        ),
        "mp",
        0,
        0,
        tiled=True,
    )
    partial_grad = local(
        subspace,
        bf16((N_MP, RANK, cols)),
        at,
        columns,
        ins=[VMEM],
        flops=2**25,
        moved=2**20,
        name="subspace",
    )

    theirs = lax.ppermute(partial_grad, "dp", SWAP)
    both = (partial_grad.astype(jnp.float32) + theirs.astype(jnp.float32)).astype(jnp.bfloat16)
    both, input_grad = lax.optimization_barrier((both, input_grad))
    input_grad = lax.psum_scatter(
        input_grad, "mp", scatter_dimension=0, axis_index_groups=GROUPS_Z, tiled=True
    )
    got = lax.all_to_all(both, "dp", 0, 0, axis_index_groups=ACROSS, tiled=True)

    packed_width = RANK // rows * first_moment.shape[1]
    new_first, new_second, packed = local(
        adam,
        (f32(first_moment.shape), f32(first_moment.shape), bf16((N_MP, rows, packed_width))),
        at,
        got,
        first_moment,
        second_moment,
        ins=[VMEM] * 3,
        flops=2**19,
        moved=2**20,
        name="adam",
    )
    update = local(
        back_project,
        bf16((first_moment.shape[1], width // N_MP)),
        at,
        mine,
        other,
        lax.all_to_all(packed, "mp", 0, 0, tiled=True),
        ins=[VMEM] * 3,
        flops=2 * 2**26,
        moved=2**21,
        name="back_project",
    )
    return (input_grad, update.T, new_first, new_second)


def solution(mesh):
    placed = (
        P(("dp", "mp"), None),
        P(None, "mp"),
        P("dp", "mp"),
        P(None, "mp"),
        P("mp", "dp"),
        P("mp", "dp"),
    )
    return jax.shard_map(
        body,
        mesh=mesh,
        in_specs=placed,
        out_specs=(P(("dp", "mp"), None), P("mp", "dp"), P("mp", "dp"), P("mp", "dp")),
        check_vma=False,
    )
```

```python
import functools

import jax
import jax.numpy as jnp
from jax import lax
from jax.experimental import pallas as pl
from jax.experimental.pallas import tpu as pltpu
from jax.sharding import PartitionSpec as P

STEP = 10


epsilon = 1e-08

X, ZH, N_MP, N_DP, RANK = 4, 4, 16, 32, 64
GROUPS_X = [[z + ZH * x for x in range(X)] for z in range(ZH)]
GROUPS_Z = [[z + ZH * x for z in range(ZH)] for x in range(X)]
ACROSS = [[2 * k + c for k in range(N_DP // 2)] for c in range(2)]
SWAP = [(d, d ^ 1) for d in range(N_DP)]
NT = (((1,), (1,)), ((), ()))
TN = (((0,), (0,)), ((), ()))
LIMIT = 48 * 2**20


VMEM = pl.BlockSpec(memory_space=pltpu.VMEM)
HBM = pl.BlockSpec(memory_space=pltpu.HBM)


def local(kernel, outs, *args, ins, scratch=(), limit=LIMIT, flops=0, moved=0, name):
    return pl.pallas_call(
        kernel,
        out_shape=outs,
        in_specs=[pl.BlockSpec(memory_space=pltpu.SMEM), *ins],
        out_specs=jax.tree.map(lambda _: VMEM, outs),
        scratch_shapes=scratch,
        compiler_params=pltpu.CompilerParams(vmem_limit_bytes=limit),
        cost_estimate=pl.CostEstimate(flops=flops, bytes_accessed=moved, transcendentals=0),
        name=name,
    )(*args)


def pack_rows(at_ref, basis_ref, tok_ref, out_ref, tok, sems):
    core = at_ref[0]
    half = out_ref.shape[2]
    first = pltpu.make_async_copy(tok_ref, tok, sems.at[0])
    first.start()
    copies = []
    for j in range(N_MP):
        mine = pl.ds(pl.multiple_of((2 * j + core) * half, half), half)
        copies.append(
            pltpu.make_async_copy(basis_ref.at[:, mine], out_ref.at[j, pl.ds(0, RANK), :], sems.at[1])
        )
    for copy in copies:
        copy.start()
    first.wait()
    for j in range(N_MP):
        mine = pl.ds(pl.multiple_of((2 * j + core) * half, half), half)
        other = pl.ds(pl.multiple_of((2 * j + 1 - core) * half, half), half)
        out_ref[j, RANK:, :] = jnp.concatenate([tok[:, mine], tok[:, other]], axis=0)
    for copy in copies:
        copy.wait()


def adam(at_ref, got_ref, first_ref, second_ref, new_first_ref, new_second_ref, out_ref):
    rank, width = first_ref.shape
    total = got_ref[0].astype(jnp.float32)
    for j in range(1, got_ref.shape[0]):
        total += got_ref[j].astype(jnp.float32)
    grad = jnp.concatenate([total[:, :width], total[:, width:]], axis=0)
    new_first = 0.9 * first_ref[...] + 0.1 * grad
    new_second = 0.999 * second_ref[...] + 0.001 * grad * grad
    new_first_ref[...] = new_first
    new_second_ref[...] = new_second
    first_scale = 1.0 - 0.9**STEP
    second_scale = 1.0 - 0.999**STEP
    direction = new_first / first_scale / (jnp.sqrt(new_second / second_scale) + epsilon)
    wide = jnp.concatenate([direction[: rank // 2], direction[rank // 2 :]], axis=1)
    rows = out_ref.shape[1]
    flat = jnp.concatenate(
        [wide[rows * b : rows * (b + 1)] for b in range(rank // 2 // rows)], axis=1
    ).astype(jnp.bfloat16)
    for j in range(N_MP):
        out_ref[j] = flat


def back_project(at_ref, mine_ref, other_ref, got_ref, update_ref):
    core = at_ref[0]
    cols, half = update_ref.shape[0], mine_ref.shape[2]
    rows = got_ref.shape[1]
    lanes = 2 * cols
    parts = []
    for j in range(N_MP):
        flat = got_ref[j].astype(jnp.float32)
        parts += [flat[:, lanes * b : lanes * (b + 1)] for b in range(RANK // 2 // rows)]
    direction = jnp.concatenate(parts, axis=0).astype(jnp.bfloat16)
    for where, ref in ((core, mine_ref), (1 - core, other_ref)):
        low = ref[:, : RANK // 2, :].reshape(N_MP * RANK // 2, half)
        high = ref[:, RANK // 2 : RANK, :].reshape(N_MP * RANK // 2, half)
        low = lax.dot_general(direction, low, TN, preferred_element_type=jnp.float32)
        high = lax.dot_general(direction, high, TN, preferred_element_type=jnp.float32)
        update_ref[:, pl.ds(pl.multiple_of(where * half, half), half)] = (
            low[:cols] + high[cols:]
        ).astype(update_ref.dtype)


def subspace(at_ref, got_ref, mine_ref, other_ref):
    core = at_ref[0]
    total = got_ref[0, :RANK, :].astype(jnp.float32)
    for j in range(1, N_MP):
        total += got_ref[j, :RANK, :].astype(jnp.float32)
    projected = total.astype(jnp.bfloat16)
    for j in range(N_MP):
        grad = jnp.dot(projected, got_ref[j, RANK:, :], preferred_element_type=jnp.float32)
        width = grad.shape[1] // 2
        low, high = grad[: RANK // 2], grad[RANK // 2 :]
        first = jnp.concatenate([low[:, :width], high[:, :width]], axis=1)
        second = jnp.concatenate([low[:, width:], high[:, width:]], axis=1)
        mine_ref[j] = jnp.where(core == 0, first, second).astype(mine_ref.dtype)
        other_ref[j] = jnp.where(core == 0, second, first).astype(other_ref.dtype)


def body(tokens, kv_weight, out_grad, basis, first_moment, second_moment):
    bf16 = functools.partial(jax.ShapeDtypeStruct, dtype=jnp.bfloat16)
    f32 = functools.partial(jax.ShapeDtypeStruct, dtype=jnp.float32)
    rows, width = tokens.shape
    half = width // N_MP // 2
    n_tok, cols = out_grad.shape
    at = (lax.axis_index("dp") & 1)[None]

    packed = local(
        pack_rows,
        bf16((N_MP, RANK + 2 * rows, half)),
        at,
        basis.T,
        tokens,
        ins=[HBM] * 2,
        scratch=[pltpu.VMEM((rows, width), jnp.bfloat16), pltpu.SemaphoreType.DMA((2,))],
        limit=60 * 2**20,
        flops=0,
        moved=2 * 2**20,
        name="pack_rows",
    )
    packed, kv_weight, out_grad = lax.optimization_barrier((packed, kv_weight, out_grad))
    mine = lax.all_to_all(packed, "mp", 0, 0, tiled=True)

    terms = lax.dot_general(
        out_grad, kv_weight, (((1,), (1,)), ((), ())), preferred_element_type=jnp.float32
    ).astype(jnp.bfloat16)
    input_grad = lax.psum_scatter(
        terms, "mp", scatter_dimension=0, axis_index_groups=GROUPS_X, tiled=True
    )

    other = lax.ppermute(mine, "dp", SWAP)

    def block(a, lo, hi):
        return a[:, lo:hi].reshape(N_MP * (hi - lo), half)

    projected = lax.dot_general(
        block(mine, 0, RANK), block(mine, RANK, RANK + rows), NT, preferred_element_type=jnp.float32
    ) + lax.dot_general(
        block(other, 0, RANK),
        block(mine, RANK + rows, RANK + 2 * rows),
        NT,
        preferred_element_type=jnp.float32,
    )
    projected = projected.astype(jnp.bfloat16).reshape(N_MP, RANK, n_tok)

    columns = lax.all_to_all(
        jnp.concatenate(
            [projected, jnp.broadcast_to(out_grad[None], (N_MP, n_tok, cols))], axis=1
        ),
        "mp",
        0,
        0,
        tiled=True,
    )
    partial_grad, theirs = local(
        subspace,
        (bf16((N_MP, RANK // 2, cols)), bf16((N_MP, RANK // 2, cols))),
        at,
        columns,
        ins=[VMEM],
        flops=2**31,
        moved=2**20,
        name="subspace",
    )

    theirs = lax.ppermute(theirs, "dp", SWAP)
    both = (partial_grad.astype(jnp.float32) + theirs.astype(jnp.float32)).astype(jnp.bfloat16)
    both, input_grad = lax.optimization_barrier((both, input_grad))
    input_grad = lax.psum_scatter(
        input_grad, "mp", scatter_dimension=0, axis_index_groups=GROUPS_Z, tiled=True
    )
    got = lax.all_to_all(both, "dp", 0, 0, axis_index_groups=ACROSS, tiled=True)

    packed_width = RANK // rows * first_moment.shape[1]
    new_first, new_second, packed = local(
        adam,
        (f32(first_moment.shape), f32(first_moment.shape), bf16((N_MP, rows, packed_width))),
        at,
        got,
        first_moment,
        second_moment,
        ins=[VMEM] * 3,
        flops=2**19,
        moved=2**20,
        name="adam",
    )
    update = local(
        back_project,
        bf16((first_moment.shape[1], width // N_MP)),
        at,
        mine,
        other,
        lax.all_to_all(packed, "mp", 0, 0, tiled=True),
        ins=[VMEM] * 3,
        flops=2 * 2**26,
        moved=2**21,
        name="back_project",
    )
    return (input_grad, update.T, new_first, new_second)


def solution(mesh):
    placed = (
        P(("dp", "mp"), None),
        P(None, "mp"),
        P("dp", "mp"),
        P(None, "mp"),
        P("mp", "dp"),
        P("mp", "dp"),
    )
    return jax.shard_map(
        body,
        mesh=mesh,
        in_specs=placed,
        out_specs=(P(("dp", "mp"), None), P("mp", "dp"), P("mp", "dp"), P("mp", "dp")),
        check_vma=False,
    )
```

```python
import functools

import jax
import jax.numpy as jnp
from jax import lax
from jax.experimental import pallas as pl
from jax.experimental.pallas import tpu as pltpu
from jax.sharding import PartitionSpec as P

STEP = 10


epsilon = 1e-08

X, ZH, N_MP, N_DP, RANK = 4, 4, 16, 32, 64
GROUPS_X = [[z + ZH * x for x in range(X)] for z in range(ZH)]
GROUPS_Z = [[z + ZH * x for z in range(ZH)] for x in range(X)]
ACROSS = [[2 * k + c for k in range(N_DP // 2)] for c in range(2)]
SWAP = [(d, d ^ 1) for d in range(N_DP)]
NT = (((1,), (1,)), ((), ()))
TN = (((0,), (0,)), ((), ()))
LIMIT = 16 * 2**20


VMEM = pl.BlockSpec(memory_space=pltpu.VMEM)
HBM = pl.BlockSpec(memory_space=pltpu.HBM)


def local(kernel, outs, *args, ins, scratch=(), limit=LIMIT, flops=0, moved=0, name):
    return pl.pallas_call(
        kernel,
        out_shape=outs,
        in_specs=[pl.BlockSpec(memory_space=pltpu.SMEM), *ins],
        out_specs=jax.tree.map(lambda _: VMEM, outs),
        scratch_shapes=scratch,
        compiler_params=pltpu.CompilerParams(vmem_limit_bytes=limit),
        cost_estimate=pl.CostEstimate(flops=flops, bytes_accessed=moved, transcendentals=0),
        name=name,
    )(*args)


def pack_rows(at_ref, basis_ref, tok_ref, out_ref, tok, sems):
    core = at_ref[0]
    half = out_ref.shape[2]
    first = pltpu.make_async_copy(tok_ref, tok, sems.at[0])
    first.start()
    copies = []
    for j in range(N_MP):
        mine = pl.ds(pl.multiple_of((2 * j + core) * half, half), half)
        copies.append(
            pltpu.make_async_copy(basis_ref.at[:, mine], out_ref.at[j, pl.ds(0, RANK), :], sems.at[1])
        )
    for copy in copies:
        copy.start()
    first.wait()
    for j in range(N_MP):
        mine = pl.ds(pl.multiple_of((2 * j + core) * half, half), half)
        other = pl.ds(pl.multiple_of((2 * j + 1 - core) * half, half), half)
        out_ref[j, RANK:, :] = jnp.concatenate([tok[:, mine], tok[:, other]], axis=0)
    for copy in copies:
        copy.wait()


def combine(at_ref, mine_ref, theirs_ref, out_ref):
    out_ref[...] = (mine_ref[...].astype(jnp.float32) + theirs_ref[...].astype(jnp.float32)).astype(
        out_ref.dtype
    )


def adam(at_ref, got_ref, parts_ref, new_first_ref, new_second_ref, out_ref):
    rank, width = parts_ref.shape[1:]
    total = got_ref[0].astype(jnp.float32)
    for j in range(1, got_ref.shape[0]):
        total += got_ref[j].astype(jnp.float32)
    grad = jnp.concatenate([total[:, :width], total[:, width:]], axis=0)
    new_first = parts_ref[0] + 0.1 * grad
    new_second = parts_ref[1] + 0.001 * grad * grad
    new_first_ref[...] = new_first
    new_second_ref[...] = new_second
    first_scale = 1.0 - 0.9**STEP
    second_scale = 1.0 - 0.999**STEP
    direction = new_first / first_scale / (jnp.sqrt(new_second / second_scale) + epsilon)
    wide = jnp.concatenate([direction[: rank // 2], direction[rank // 2 :]], axis=1)
    rows = out_ref.shape[1]
    flat = jnp.concatenate(
        [wide[rows * b : rows * (b + 1)] for b in range(rank // 2 // rows)], axis=1
    ).astype(jnp.bfloat16)
    for j in range(N_MP):
        out_ref[j] = flat


def back_project(at_ref, mine_ref, other_ref, got_ref, update_ref):
    core = at_ref[0]
    cols, half = update_ref.shape[0], mine_ref.shape[2]
    rows = got_ref.shape[1]
    lanes = 2 * cols
    parts = []
    for j in range(N_MP):
        flat = got_ref[j].astype(jnp.float32)
        parts += [flat[:, lanes * b : lanes * (b + 1)] for b in range(RANK // 2 // rows)]
    direction = jnp.concatenate(parts, axis=0).astype(jnp.bfloat16)
    for where, ref in ((core, mine_ref), (1 - core, other_ref)):
        low = ref[:, : RANK // 2, :].reshape(N_MP * RANK // 2, half)
        high = ref[:, RANK // 2 : RANK, :].reshape(N_MP * RANK // 2, half)
        low = lax.dot_general(direction, low, TN, preferred_element_type=jnp.float32)
        high = lax.dot_general(direction, high, TN, preferred_element_type=jnp.float32)
        update_ref[:, pl.ds(pl.multiple_of(where * half, half), half)] = (
            low[:cols] + high[cols:]
        ).astype(update_ref.dtype)


def subspace(at_ref, got_ref, mine_ref, other_ref):
    core = at_ref[0]
    total = got_ref[0, :RANK, :].astype(jnp.float32)
    for j in range(1, N_MP):
        total += got_ref[j, :RANK, :].astype(jnp.float32)
    projected = total.astype(jnp.bfloat16)
    for j in range(N_MP):
        grad = jnp.dot(projected, got_ref[j, RANK:, :], preferred_element_type=jnp.float32)
        width = grad.shape[1] // 2
        low, high = grad[: RANK // 2], grad[RANK // 2 :]
        first = jnp.concatenate([low[:, :width], high[:, :width]], axis=1)
        second = jnp.concatenate([low[:, width:], high[:, width:]], axis=1)
        mine_ref[j] = jnp.where(core == 0, first, second).astype(mine_ref.dtype)
        other_ref[j] = jnp.where(core == 0, second, first).astype(other_ref.dtype)


def body(tokens, kv_weight, out_grad, basis, first_moment, second_moment):
    bf16 = functools.partial(jax.ShapeDtypeStruct, dtype=jnp.bfloat16)
    f32 = functools.partial(jax.ShapeDtypeStruct, dtype=jnp.float32)
    rows, width = tokens.shape
    half = width // N_MP // 2
    n_tok, cols = out_grad.shape
    at = (lax.axis_index("dp") & 1)[None]

    packed = local(
        pack_rows,
        bf16((N_MP, RANK + 2 * rows, half)),
        at,
        basis.T,
        tokens,
        ins=[HBM] * 2,
        scratch=[pltpu.VMEM((rows, width), jnp.bfloat16), pltpu.SemaphoreType.DMA((2,))],
        limit=60 * 2**20,
        flops=0,
        moved=2 * 2**20,
        name="pack_rows",
    )
    packed, kv_weight, out_grad = lax.optimization_barrier((packed, kv_weight, out_grad))
    mine = lax.all_to_all(packed, "mp", 0, 0, tiled=True)

    terms = lax.dot_general(
        out_grad, kv_weight, (((1,), (1,)), ((), ())), preferred_element_type=jnp.float32
    ).astype(jnp.bfloat16)
    input_grad = lax.psum_scatter(
        terms, "mp", scatter_dimension=0, axis_index_groups=GROUPS_X, tiled=True
    )

    other = lax.ppermute(mine, "dp", SWAP)

    def block(a, lo, hi):
        return a[:, lo:hi].reshape(N_MP * (hi - lo), half)

    projected = lax.dot_general(
        block(mine, 0, RANK), block(mine, RANK, RANK + rows), NT, preferred_element_type=jnp.float32
    ) + lax.dot_general(
        block(other, 0, RANK),
        block(mine, RANK + rows, RANK + 2 * rows),
        NT,
        preferred_element_type=jnp.float32,
    )
    projected = projected.astype(jnp.bfloat16).reshape(N_MP, RANK, n_tok)

    columns = lax.all_to_all(
        jnp.concatenate(
            [projected, jnp.broadcast_to(out_grad[None], (N_MP, n_tok, cols))], axis=1
        ),
        "mp",
        0,
        0,
        tiled=True,
    )
    partial_grad, theirs = local(
        subspace,
        (bf16((N_MP, RANK // 2, cols)), bf16((N_MP, RANK // 2, cols))),
        at,
        columns,
        ins=[VMEM],
        flops=2**32,
        moved=2**20,
        name="subspace",
    )

    partial_grad, theirs, first_moment, second_moment = lax.optimization_barrier(
        (partial_grad, theirs, first_moment, second_moment)
    )
    theirs = lax.ppermute(theirs, "dp", SWAP)

    parts = jnp.stack([0.9 * first_moment, 0.999 * second_moment])
    theirs, parts = lax.optimization_barrier((theirs, parts))
    both = local(
        combine,
        bf16(partial_grad.shape),
        at,
        partial_grad,
        theirs,
        ins=[VMEM] * 2,
        flops=2**16,
        moved=2**18,
        name="combine",
    )
    both, input_grad = lax.optimization_barrier((both, input_grad))
    input_grad = lax.psum_scatter(
        input_grad, "mp", scatter_dimension=0, axis_index_groups=GROUPS_Z, tiled=True
    )
    got = lax.all_to_all(both, "dp", 0, 0, axis_index_groups=ACROSS, tiled=True)

    packed_width = RANK // rows * first_moment.shape[1]
    new_first, new_second, packed = local(
        adam,
        (f32(first_moment.shape), f32(first_moment.shape), bf16((N_MP, rows, packed_width))),
        at,
        got,
        parts,
        ins=[VMEM] * 2,
        flops=2**19,
        moved=2**20,
        name="adam",
    )
    update = local(
        back_project,
        bf16((first_moment.shape[1], width // N_MP)),
        at,
        mine,
        other,
        lax.all_to_all(packed, "mp", 0, 0, tiled=True),
        ins=[VMEM] * 3,
        flops=2 * 2**26,
        moved=2**21,
        name="back_project",
    )
    return (input_grad, update.T, new_first, new_second)


def solution(mesh):
    placed = (
        P(("dp", "mp"), None),
        P(None, "mp"),
        P("dp", "mp"),
        P(None, "mp"),
        P("mp", "dp"),
        P("mp", "dp"),
    )
    return jax.shard_map(
        body,
        mesh=mesh,
        in_specs=placed,
        out_specs=(P(("dp", "mp"), None), P("mp", "dp"), P("mp", "dp"), P("mp", "dp")),
        check_vma=False,
    )
```
